32 devices in a mesh: gx: 4 (over y, core), gy: 4 (over z), gz: 2 (over x).
Axes of the slice: x: 2, y: 2, z: 4, core: 2. Of those that a mesh axis runs over, the one named last changes fastest.
Arguments:
- positions: float32 [3, 4096], P(None, ('gx', 'gy', 'gz')), as said below
- attributes: float32 [128, 4096], P(None, ('gx', 'gy', 'gz')), may hold values from -6 to 6
- species: int32 [4096], P(('gx', 'gy', 'gz')), may hold values from 0 to 3
- occupied: int32 [4096], P(('gx', 'gy', 'gz')), may hold values from 0 to 1
- neighbours: int32 [32, 4096], P(None, ('gx', 'gy', 'gz')), may hold values from 0 to 977, as said below
- pair_flags: int32 [32, 4096], P(None, ('gx', 'gy', 'gz')), may hold values from 0 to 1, as said below
- site_slots: int32 [4096], P(('gx', 'gy', 'gz')), may hold values from 0 to 127, as said below
- radial_weight: float32 [8, 64], replicated, may hold values from -2 to 2
- node_weight: float32 [128, 128], replicated, may hold values from -0.5 to 0.5
- mix_weight: float32 [64, 128], replicated, may hold values from -0.75 to 0.75
- latent_in: float32 [256, 128], replicated, may hold values from -0.375 to 0.375
- latent_out: float32 [128, 64], replicated, may hold values from -0.5 to 0.5
- readout: float32 [64], replicated, may hold values from -0.75 to 0.75
- species_scale: float32 [4], replicated, may hold values from 0.5 to 1.5
- species_shift: float32 [4], replicated, may hold values from -3 to 3
Outputs:
- atom_energy: float32 [4096], P(('gx', 'gy', 'gz'))
- forces: float32 [3, 4096], P(None, ('gx', 'gy', 'gz'))
The draws below stay inside these ranges and needn't reach their ends.
Inputs may be any that keep to these rules, and one draw needn't show every extreme that they name: `positions`: atoms sit on a jittered lattice of 8 x 8 x 2 sites a brick, spacing 1.5 angstrom; every coordinate lies inside its brick. Each atom's 32 slots name the lattice neighbours at integer site offsets of length 1 to 2, in an order rotated for each atom; every named atom lies within 4 angstrom of the centre after the image shift; a code of 128 or more names a site outside the brick, numbered as in the reference program. `pair_flags`: A flag is 1 exactly where the centre and the named atom are both occupied. `site_slots`: within each brick every slot appears once, in an order drawn for each brick.
All inputs are finite; a program needn't handle non-finite values.
Results may differ from the reference program's by a relative error of at most 0.0003.
Values sent between devices are 32-bit elements; how exact they have to be, the bound alone decides.
A program may use at most 64 MiB of HBM per device.

```python
import math
import jax
import jax.numpy as jnp
import numpy as np
from jax import lax

CH = 64
HID = 128
ATTR = 128
NB = 8
SPECIES = 4
K = 32
LXY = 8
LZ = 2
A_DEV = 128
BRICKS_X = 4
BRICKS_Y = 4
BRICKS_Z = 2
NATOMS = 4096
DEVICES = 32


SPACING = 1.5


def device_count():
    return BRICKS_X * BRICKS_Y * BRICKS_Z


def offset_list():
    chosen = [[dx, dy, dz] for dx in range(-2, 3) for dy in range(-2, 3) for dz in range(-2, 3) if 0 < dx * dx + dy * dy + dz * dz <= 4]
    return jnp.asarray(np.array(chosen, dtype=np.int32).T)


def shuffle_one(subkey):
    return jax.random.permutation(subkey, A_DEV)


def lattice(key):
    bricks = device_count()
    subkeys = jax.random.split(jax.random.fold_in(key, 11), bricks)
    slot_of_site = jax.vmap(shuffle_one)(subkeys).astype(jnp.int32)
    brick_rows = jnp.arange(bricks, dtype=jnp.int32)[:, None]
    site_ids = jnp.broadcast_to(jnp.arange(A_DEV, dtype=jnp.int32)[None, :], (bricks, A_DEV))
    site_of_slot = jnp.zeros((bricks, A_DEV), jnp.int32).at[brick_rows, slot_of_site].set(site_ids)
    present = (jax.random.randint(jax.random.fold_in(key, 12), (bricks, A_DEV), 0, 8) > 0).astype(jnp.int32)
    return (slot_of_site, site_of_slot, present)


def wiring(key):
    slot_of_site, site_of_slot, present = lattice(key)
    bricks = device_count()
    turn = jax.random.randint(jax.random.fold_in(key, 13), (bricks, A_DEV), 0, K)
    offsets = offset_list()
    pick = (jnp.arange(K, dtype=jnp.int32)[:, None, None] + turn[None]) % K
    delta = offsets[:, pick]
    site = site_of_slot[None]
    extents = jnp.array([LXY, LXY, LZ], jnp.int32)[:, None, None, None]
    coords = jnp.stack([site // (LXY * LZ), site // LZ % LXY, site % LZ])
    target = coords + delta
    image = jnp.floor_divide(target, extents)
    inside = target - image * extents
    brick_ids = jnp.arange(bricks, dtype=jnp.int32)
    brick_pos = jnp.stack([brick_ids // (BRICKS_Y * BRICKS_Z), brick_ids // BRICKS_Z % BRICKS_Y, brick_ids % BRICKS_Z])[:, None, :, None]
    counts = jnp.array([BRICKS_X, BRICKS_Y, BRICKS_Z], jnp.int32)[:, None, None, None]
    moved = (brick_pos + image) % counts
    sender = (moved[0] * BRICKS_Y + moved[1]) * BRICKS_Z + moved[2]
    target_site = (inside[0] * LXY + inside[1]) * LZ + inside[2]
    target_slot = slot_of_site[sender, target_site]
    wide_cell = ((target[0] + 2) * (LXY + 4) + target[1] + 2) * (LZ + 4) + target[2] + 2
    local_flag = jnp.all(image == 0, axis=0)
    codes = jnp.where(local_flag, target_slot, A_DEV + wide_cell)
    neighbour_global = sender * A_DEV + target_slot
    return (codes, neighbour_global, present)


def draw_positions(key, part):
    slot_of_site, site_of_slot, present = lattice(key)
    key = jax.random.fold_in(key, 4)
    bricks = device_count()
    site = site_of_slot[None]
    coords = jnp.stack([site // (LXY * LZ), site // LZ % LXY, site % LZ])[:, 0].astype(jnp.float32)
    spread = 0.25
    jitter = jax.random.uniform(key, (3, bricks, A_DEV), jnp.float32, -spread, spread)
    values = SPACING * (coords + 0.5) + jitter
    return values.reshape(3, bricks * A_DEV)


def draw_occupied(key, part):
    slot_of_site, site_of_slot, present = lattice(key)
    key = jax.random.fold_in(key, 5)
    return present.reshape(-1)


def draw_neighbours(key, part):
    codes, neighbour_global, present = wiring(key)
    key = jax.random.fold_in(key, 6)
    return codes.reshape(K, -1).astype(jnp.int32)


def draw_pair_flags(key, part):
    codes, neighbour_global, present = wiring(key)
    key = jax.random.fold_in(key, 7)
    flags = present[None] * present.reshape(-1)[neighbour_global]
    return flags.reshape(K, -1).astype(jnp.int32)


def draw_site_slots(key, part):
    slot_of_site, site_of_slot, present = lattice(key)
    key = jax.random.fold_in(key, 8)
    return slot_of_site.reshape(-1).astype(jnp.int32)


def with_ends(values, key, smallest, high):
    dims = values.shape
    index_at = [jax.random.randint(jax.random.fold_in(key, axis), (), 0, dims[axis]) for axis in range(len(dims))]
    values = values.at[tuple(index_at)].set(smallest)
    longest = dims.index(max(dims))
    index_at[longest] = (index_at[longest] + 1) % dims[longest]
    return values.at[tuple(index_at)].set(high)


def steps_of(stream_key, dims, cuts, least, high):
    loudness = 1.0
    for axis_at, shards_of in cuts:
        steps = jax.random.uniform(jax.random.fold_in(jax.random.fold_in(stream_key, 6), axis_at), (shards_of,), jnp.float32, least / len(cuts), high / len(cuts))
        loudness = loudness * jnp.repeat(jnp.exp(steps), dims[axis_at] // shards_of).reshape((-1,) + (1,) * (len(dims) - 1 - axis_at))
    return loudness


def noise(rng, shape, scale, limit, cuts=(), kind=jnp.bfloat16):
    result = jax.random.normal(rng, shape, jnp.float32) * scale
    if len(cuts) > 0:
        result = steps_of(rng, shape, cuts, -0.22, 0.18) * result
    return jnp.clip(result, min=-limit, max=limit).astype(kind)


def setup_inputs(seed: int = 0) -> dict:
    splits = jax.random.split(jax.random.key(seed), 16)
    return {
        "positions": draw_positions(jax.random.fold_in(splits[15], 71), 0),
        "attributes": noise(splits[1], (ATTR, NATOMS), 1.0, 6.0, ((1, 32),), jnp.float32),
        "species": with_ends(jax.random.randint(splits[2], (NATOMS,), 0, SPECIES), jax.random.fold_in(splits[2], 1), 0, SPECIES - 1).astype(jnp.int32),
        "occupied": draw_occupied(jax.random.fold_in(splits[15], 71), 0),
        "neighbours": draw_neighbours(jax.random.fold_in(splits[15], 71), 0),
        "pair_flags": draw_pair_flags(jax.random.fold_in(splits[15], 71), 0),
        "site_slots": draw_site_slots(jax.random.fold_in(splits[15], 71), 0),
        "radial_weight": noise(splits[7], (NB, CH), NB ** -0.5, 2.0, (), jnp.float32),
        "node_weight": noise(splits[8], (ATTR, 2 * CH), ATTR ** -0.5, 0.5, (), jnp.float32),
        "mix_weight": noise(splits[9], (CH, 2 * CH), CH ** -0.5, 0.75, (), jnp.float32),
        "latent_in": noise(splits[10], (4 * CH, HID), (4 * CH) ** -0.5, 0.375, (), jnp.float32),
        "latent_out": noise(splits[11], (HID, CH), HID ** -0.5, 0.5, (), jnp.float32),
        "readout": noise(splits[12], (CH,), CH ** -0.5, 0.75, (), jnp.float32),
        "species_scale": jnp.clip(1.0 + 0.1 * jax.random.normal(splits[13], (SPECIES,), jnp.float32), 0.5, 1.5),
        "species_shift": noise(splits[14], (SPECIES,), 1.0, 3.0, (), jnp.float32),
    }


SPACING = 1.5
CUTOFF = 4.0
PRECISE = lax.Precision.HIGHEST
ROOT_THREE = math.sqrt(3.0)
ROOT_FIVE = math.sqrt(5.0)
ROOT_FIFTEEN = math.sqrt(15.0)

def harmonics(separation):
    distance = jnp.sqrt(lax.optimization_barrier(jnp.sum(separation * separation, axis=0)))
    direction = separation / distance
    along_x, along_y, along_z = (direction[0], direction[1], direction[2])
    harmonic = jnp.stack([jnp.ones_like(along_x), ROOT_THREE * along_x, ROOT_THREE * along_y, ROOT_THREE * along_z, ROOT_FIFTEEN * along_x * along_y, ROOT_FIFTEEN * along_y * along_z, 0.5 * ROOT_FIVE * (3.0 * along_z * along_z - 1.0), ROOT_FIFTEEN * along_x * along_z, 0.5 * ROOT_FIFTEEN * (along_x * along_x - along_y * along_y)])
    return (distance, harmonic)

def pair_model(separation, center, near_term, flag_values, species_row, present, radial_weight, mix_weight, latent_in, latent_out, readout, species_scale, species_shift):
    distance, harmonic = harmonics(separation)
    scaled = distance / CUTOFF
    envelope = (1.0 - scaled * scaled) * (1.0 - scaled * scaled) * flag_values
    degree = jnp.arange(1, radial_weight.shape[0] + 1).astype(jnp.float32)
    radial = jnp.sin(degree[:, None, None] * (math.pi / CUTOFF) * distance[None]) / distance[None]
    summed = jnp.einsum('bc,bka->cka', radial_weight, radial, precision=PRECISE) + center[:, None, :] + near_term
    first_latent = jax.nn.silu(summed)
    channels = first_latent.shape[0]
    mixture = jnp.einsum('cf,cka->fka', mix_weight, first_latent, precision=PRECISE)
    gains = mixture[:channels]
    weighted = mixture[channels:] * envelope[None]
    slot_count = separation.shape[1]
    surroundings = jnp.einsum('cka,mka->cma', weighted, harmonic, precision=PRECISE) / math.sqrt(slot_count)
    scalar_zero = gains * jnp.einsum('mka,cma->cka', harmonic[0:1], surroundings[:, 0:1], precision=PRECISE)
    scalar_one = gains * jnp.einsum('mka,cma->cka', harmonic[1:4], surroundings[:, 1:4], precision=PRECISE)
    scalar_two = gains * jnp.einsum('mka,cma->cka', harmonic[4:9], surroundings[:, 4:9], precision=PRECISE)
    features = jnp.concatenate([first_latent, scalar_zero, scalar_one, scalar_two], axis=0)
    hidden = jax.nn.silu(jnp.einsum('fh,fka->hka', latent_in, features, precision=PRECISE))
    second_latent = first_latent + jnp.einsum('hc,hka->cka', latent_out, hidden, precision=PRECISE)
    pair_energy = jnp.einsum('c,cka->ka', readout, second_latent, precision=PRECISE) * envelope
    kinds = jnp.arange(species_scale.shape[0]).astype(jnp.int32)
    species_hot = (species_row[None, :] == kinds[:, None]).astype(jnp.float32)
    atom_scale = jnp.einsum('s,sa->a', species_scale, species_hot, precision=PRECISE)
    atom_shift = jnp.einsum('s,sa->a', species_shift, species_hot, precision=PRECISE)
    return present * (atom_scale * lax.optimization_barrier(jnp.sum(pair_energy, axis=0)) + atom_shift)

def reference(positions, attributes, species, occupied, neighbours, pair_flags, site_slots, radial_weight, node_weight, mix_weight, latent_in, latent_out, readout, species_scale, species_shift):
    atom_count = A_DEV
    wide_y = LXY + 4
    wide_z = LZ + 4
    channels = mix_weight.shape[0]
    node_terms = jnp.einsum('fc,fa->ca', node_weight, attributes, precision=PRECISE)
    center_all = node_terms[:channels]
    near_all = node_terms[channels:]
    brick_edge = jnp.array([LXY * SPACING, LXY * SPACING, LZ * SPACING], jnp.float32)

    def one_brick(forces, device):
        first_atom = device * atom_count
        center_pos = lax.dynamic_slice_in_dim(positions, first_atom, atom_count, 1)
        center = lax.dynamic_slice_in_dim(center_all, first_atom, atom_count, 1)
        species_row = lax.dynamic_slice_in_dim(species, first_atom, atom_count, 0)
        present = lax.dynamic_slice_in_dim(occupied, first_atom, atom_count, 0).astype(jnp.float32)
        neighbour_code = lax.dynamic_slice_in_dim(neighbours, first_atom, atom_count, 1)
        flag_values = lax.dynamic_slice_in_dim(pair_flags, first_atom, atom_count, 1).astype(jnp.float32)
        remote_flag = neighbour_code >= atom_count
        cell = jnp.where(remote_flag, neighbour_code - atom_count, 0)
        site_x = cell // (wide_y * wide_z) - 2
        site_y = cell // wide_z % wide_y - 2
        site_z = cell % wide_z - 2
        image_x = jnp.floor_divide(site_x, LXY)
        image_y = jnp.floor_divide(site_y, LXY)
        image_z = jnp.floor_divide(site_z, LZ)
        inside = ((site_x - image_x * LXY) * LXY + (site_y - image_y * LXY)) * LZ + (site_z - image_z * LZ)
        offset_x = jnp.where(remote_flag, image_x, 0)
        offset_y = jnp.where(remote_flag, image_y, 0)
        offset_z = jnp.where(remote_flag, image_z, 0)
        brick_x = device // (BRICKS_Y * BRICKS_Z)
        brick_y = device // BRICKS_Z % BRICKS_Y
        brick_z = device % BRICKS_Z
        sender = ((brick_x + offset_x) % BRICKS_X * BRICKS_Y + (brick_y + offset_y) % BRICKS_Y) * BRICKS_Z + (brick_z + offset_z) % BRICKS_Z
        remote = site_slots[sender * atom_count + inside] + sender * atom_count
        global_id = jnp.where(remote_flag, remote, neighbour_code + first_atom).astype(jnp.int32)
        image_shift = jnp.stack([offset_x, offset_y, offset_z]).astype(jnp.float32) * brick_edge[:, None, None]
        separation = positions[:, global_id] + image_shift - center_pos[:, None, :]
        near_term = near_all[:, global_id]

        def energy_of(pair_vectors):
            return pair_model(pair_vectors, center, near_term, flag_values, species_row, present, radial_weight, mix_weight, latent_in, latent_out, readout, species_scale, species_shift)
        energies, pullback = jax.vjp(energy_of, separation)
        gradient, = pullback(jnp.ones_like(energies))
        own_ids = first_atom + jnp.arange(atom_count).astype(jnp.int32)
        forces = forces.at[:, own_ids].add(lax.optimization_barrier(jnp.sum(gradient, axis=1)))
        forces = forces.at[:, global_id.reshape(-1)].add(-gradient.reshape(3, -1))
        return (forces, energies)
    forces, energies = lax.scan(one_brick, jnp.zeros((3, NATOMS), jnp.float32), jnp.arange(DEVICES).astype(jnp.int32))
    return (energies.reshape(-1), forces)
```

```python
import functools
import math

import jax
import jax.numpy as jnp
import numpy as np
from jax import lax
from jax.experimental import pallas as pl
from jax.experimental.pallas import tpu as pltpu
from jax.sharding import PartitionSpec as P

LXY = 8
LZ = 2
SITES = LXY * LXY * LZ
SPACING = 1.5
CUTOFF = 4.0
PRECISE = lax.Precision.HIGHEST
R3 = math.sqrt(3.0)
R5 = math.sqrt(5.0)
R15 = math.sqrt(15.0)
AXES = ("gx", "gy", "gz")
F32 = jnp.float32
BF16 = jnp.bfloat16
NT = (((1,), (1,)), ((), ()))
VMEM = pl.BlockSpec(memory_space=pltpu.VMEM)
SMEM = pl.BlockSpec(memory_space=pltpu.SMEM)


def offsets():
    span = range(-2, 3)
    return [
        (dx, dy, dz)
        for dx in span
        for dy in span
        for dz in span
        if 0 < dx * dx + dy * dy + dz * dz <= 4
    ]


def flat(x, y, z):
    return (x * LXY + y) * LZ + z


def lattice_plan(z_bricks):
    z_sides = [1] if z_bricks == 2 else [1, -1]
    groups = {}
    cursor = [SITES]

    def near(side, deep):
        if side == 0:
            return range(LXY)
        if side > 0:
            return range(0, 2 if deep else 1)
        return range(LXY - (2 if deep else 1), LXY)

    def add(o):
        lone = sum(c != 0 for c in o) == 1
        sites = [flat(x, y, z) for x in near(o[0], lone) for y in near(o[1], lone) for z in range(LZ)]
        groups[o] = (cursor[0], sites)
        cursor[0] += -(-len(sites) // 8) * 8

    for o in [(1, 0, 0), (-1, 0, 0), (0, 1, 0), (0, -1, 0)]:
        add(o)
    for oz in z_sides:
        add((0, 0, oz))
    for ox in (1, -1):
        for oy in (1, -1):
            add((ox, oy, 0))
    for oz in z_sides:
        for side in (1, -1):
            add((side, 0, oz))
            add((0, side, oz))
        for ox in (1, -1):
            for oy in (1, -1):
                add((ox, oy, oz))
    rows = -(-cursor[0] // 256) * 256
    select = np.zeros((rows, SITES), np.float32)
    for start, sites in groups.values():
        for n, site in enumerate(sites):
            select[start + n, site] = 1.0
    ds = offsets()
    hot = np.zeros((len(ds), rows, SITES), np.float32)
    shift = np.zeros((3, len(ds), SITES), np.float32)
    edge = (LXY * SPACING, LXY * SPACING, LZ * SPACING)
    for k, d in enumerate(ds):
        for x in range(LXY):
            for y in range(LXY):
                for z in range(LZ):
                    t = (x + d[0], y + d[1], z + d[2])
                    o = (t[0] // LXY, t[1] // LXY, t[2] // LZ)
                    inside = flat(t[0] % LXY, t[1] % LXY, t[2] % LZ)
                    s = flat(x, y, z)
                    for c in range(3):
                        shift[c, k, s] = o[c] * edge[c]
                    if o == (0, 0, 0):
                        g = inside
                    else:
                        key = (o[0], o[1], abs(o[2])) if z_bricks == 2 else o
                        start, sites = groups[key]
                        g = start + sites.index(inside)
                    hot[k, g, s] = 1.0
    count = len(ds) // 2
    hot = np.concatenate([hot[0::2], hot[1::2]], axis=2)
    assert hot.shape == (count, rows, 2 * SITES)
    return groups, select, hot, shift


def device_at(o, sizes):
    return tuple(
        lax.rem(lax.axis_index(a) + (c + n), n) if c else lax.axis_index(a)
        for a, c, n in zip(AXES, o, sizes)
    )


def greet(groups, sizes):
    barrier = pltpu.get_barrier_semaphore()
    for o in groups:
        pl.semaphore_signal(
            barrier, inc=1, device_id=device_at(o, sizes), device_id_type=pl.DeviceIdType.MESH
        )
    return barrier


def dot(a, b):
    return jnp.dot(a, b, preferred_element_type=F32)


def exact(a, b):
    return jnp.dot(a, b, precision=PRECISE, preferred_element_type=F32)


def halves(x):
    high = x.astype(BF16)
    return high, (x - high.astype(F32)).astype(BF16)


def stack_rhs(x):
    high, low = halves(x)
    return jnp.concatenate([high, low, high], axis=0)


def stack_lhs(w):
    high = w.astype(BF16).astype(F32)
    return jnp.concatenate([high, high, w - high], axis=1).astype(BF16)


def slot_site(row):
    slot = lax.broadcasted_iota(jnp.int32, (SITES, SITES), 0)
    return jnp.where(slot == row, 1.0, 0.0).astype(F32)


def ghosts_kernel(
    groups, sizes, rows, scale_ref, shift_ref, pos_ref, attr_ref, species_ref, occ_ref, slots_ref,
    node_ref, select_ref, own_ref, table_ref, send_buf, recv_buf, send_sem, recv_sem,
):
    used = max(start + -(-len(sites) // 8) * 8 for start, sites in groups.values())
    if used < rows:
        recv_buf[used - SITES :, :] = jnp.zeros((rows - used, SITES), F32)
    barrier = greet(groups, sizes)
    terms = exact(node_ref[...].T, attr_ref[...])
    occ = occ_ref[...].astype(F32)
    species = species_ref[...]
    scale = jnp.zeros_like(occ)
    shift = jnp.zeros_like(occ)
    for n in range(scale_ref.shape[0]):
        scale = jnp.where(species == n, scale_ref[n], scale)
        shift = jnp.where(species == n, shift_ref[n], shift)
    extra = jnp.concatenate(
        [pos_ref[...], occ, occ * scale, occ * shift, jnp.zeros((2, SITES), F32)], axis=0
    )
    data = jnp.concatenate([terms, extra], axis=0)
    data = exact(data, slot_site(slots_ref[...]))
    ch = terms.shape[0] // 2
    own_ref[...] = data
    sent = jnp.concatenate([data[ch:], jnp.zeros((SITES - ch - 8, SITES), F32)], axis=0)
    wide = exact(select_ref[...], sent.T)
    send_buf[...] = wide
    pl.semaphore_wait(barrier, len(groups))
    copies = []
    for n, (o, (start, sites)) in enumerate(groups.items()):
        back = tuple(-c for c in o)
        part = pl.ds(start - SITES, -(-len(sites) // 8) * 8)
        copies.append(
            pltpu.make_async_remote_copy(
                src_ref=send_buf.at[part],
                dst_ref=recv_buf.at[part],
                send_sem=send_sem.at[n],
                recv_sem=recv_sem.at[n],
                device_id=device_at(back, sizes),
                device_id_type=pl.DeviceIdType.MESH,
            )
        )
    for copy in copies:
        copy.start()
    for copy in copies:
        copy.wait()

    for t in range(rows // SITES):
        if t == 0:
            near, q = data[ch : 2 * ch], data[2 * ch :]
        else:
            block = recv_buf[(t - 1) * SITES : t * SITES, :].T
            near, q = block[:ch], block[ch : ch + 8]
        near_high = near.astype(BF16).astype(F32)
        q1 = q.astype(BF16).astype(F32)
        q2 = (q - q1).astype(BF16).astype(F32)
        table_ref[:, t * SITES : (t + 1) * SITES] = jnp.concatenate(
            [near_high, near - near_high, q1, q2, q - q1 - q2, jnp.zeros_like(q)], axis=0
        ).astype(BF16)


def sigmoid(v):
    return 1.0 / (1.0 + jnp.exp(-v))


def model_kernel(
    slots, ch, own_ref, table_ref, hot_ref, shift_ref, radial_ref, mix_ref, in_ref, out_w_ref,
    readout_ref, result_ref, near_s, q_s, basis_s, y_s, env_s, first_s, sig_s, gain_s, raw_s, s_s,
    ds_s, dt_s, dfirst_s, dgain_s, scal_s, dbasis_s, dy_s, g_s, lin_s, linb_s,
):
    pairs = slots // 2
    inv_root = 1.0 / math.sqrt(slots)
    table = table_ref[...]

    def fetch(p, carry):
        got = dot(table, hot_ref[p])
        for j in range(2):
            k = 2 * p + j
            part = got[:, j * SITES : (j + 1) * SITES]
            near_s[k] = part[:ch] + part[ch : 2 * ch]
            q = 2 * ch
            q_s[k] = part[q : q + 8] + part[q + 8 : q + 16] + part[q + 16 : q + 24]
        return carry

    lax.fori_loop(0, pairs, fetch, 0)

    extra = own_ref[2 * ch : 2 * ch + 8]
    ebar = extra[4:5]
    rx = (q_s[:, 0, :] + shift_ref[0]) - extra[0:1]
    ry = (q_s[:, 1, :] + shift_ref[1]) - extra[1:2]
    rz = (q_s[:, 2, :] + shift_ref[2]) - extra[2:3]
    flag = q_s[:, 3, :] * extra[3:4]
    d = jnp.sqrt(rx * rx + ry * ry + rz * rz)
    inv = 1.0 / d
    ux, uy, uz = rx * inv, ry * inv, rz * inv
    y_s[:, 0, :] = jnp.ones_like(ux)
    y_s[:, 1, :] = R3 * ux
    y_s[:, 2, :] = R3 * uy
    y_s[:, 3, :] = R3 * uz
    y_s[:, 4, :] = R15 * ux * uy
    y_s[:, 5, :] = R15 * uy * uz
    y_s[:, 6, :] = 0.5 * R5 * (3.0 * uz * uz - 1.0)
    y_s[:, 7, :] = R15 * ux * uz
    y_s[:, 8, :] = 0.5 * R15 * (ux * ux - uy * uy)
    scaled = d * (1.0 / CUTOFF)
    base = 1.0 - scaled * scaled
    env_s[...] = base * base * flag
    denv_dd = base * scaled * flag * (-4.0 / CUTOFF)
    angle = d * (math.pi / CUTOFF)
    sines = [jnp.sin(angle)]
    cosines = [jnp.cos(angle)]
    for n in range(1, radial_ref.shape[0]):
        sines.append(sines[0] * cosines[-1] + cosines[0] * sines[-1])
        cosines.append(cosines[0] * cosines[-1] - sines[0] * sines[n - 1])
    for n in range(radial_ref.shape[0]):
        basis_s[:, n, :] = sines[n] * inv

    centre = own_ref[:ch]
    radial_t = radial_ref[...].T
    mix3_t = stack_lhs(mix_ref[...].T)

    def first(p, carry):
        basis = jnp.concatenate([basis_s[2 * p], basis_s[2 * p + 1]], axis=1)
        radial = exact(radial_t, basis)
        total = []
        for j in range(2):
            k = 2 * p + j
            v = radial[:, j * SITES : (j + 1) * SITES] + centre + near_s[k]
            sig = sigmoid(v)
            act = v * sig
            first_s[k] = act
            sig_s[k] = sig * (1.0 + v * (1.0 - sig))
            total.append(act)
        mixture = dot(mix3_t, stack_rhs(jnp.concatenate(total, axis=1)))
        for j in range(2):
            k = 2 * p + j
            part = mixture[:, j * SITES : (j + 1) * SITES]
            gain_s[k] = part[:ch]
            raw_s[k] = part[ch:]
        return carry

    lax.fori_loop(0, pairs, first, 0)

    step = 16
    for c in range(0, ch, step):

        def gather_s(k, acc):
            w = raw_s[k, c : c + step, :] * env_s[pl.ds(k, 1), :]
            return tuple(a + w * (y_s[k, m : m + 1, :]) if m else a + w for m, a in enumerate(acc))

        acc = lax.fori_loop(
            0, slots, gather_s, tuple(jnp.zeros((step, SITES), F32) for _ in range(9)), unroll=4
        )
        for m in range(9):
            s_s[m, c : c + step, :] = acc[m] * inv_root

    lin_s[...] = stack_lhs(in_ref[...].T)
    linb_s[...] = stack_lhs(in_ref[...])
    readout_row = readout_ref[...]
    v_col = jnp.sum(out_w_ref[...] * readout_row, axis=1, keepdims=True)
    same = lax.broadcasted_iota(jnp.int32, (ch, ch), 0) == lax.broadcasted_iota(jnp.int32, (ch, ch), 1)
    r_col = jnp.sum(jnp.where(same, readout_row, 0.0), axis=1, keepdims=True)

    def middle(p, energy):
        feats, gains, t1s, t2s, envs = [], [], [], [], []
        for j in range(2):
            k = 2 * p + j
            y = [y_s[k, m : m + 1, :] for m in range(9)]
            t1 = y[1] * s_s[1]
            for m in (2, 3):
                t1 = t1 + y[m] * s_s[m]
            t2 = y[4] * s_s[4]
            for m in (5, 6, 7, 8):
                t2 = t2 + y[m] * s_s[m]
            gain = gain_s[k]
            feats.append(jnp.concatenate([first_s[k], gain * s_s[0], gain * t1, gain * t2], axis=0))
            gains.append(gain)
            t1s.append(t1)
            t2s.append(t2)
            envs.append(env_s[pl.ds(k, 1), :])
        hidden = dot(lin_s[...], stack_rhs(jnp.concatenate(feats, axis=1)))
        sig = sigmoid(hidden)
        act = hidden * sig
        slope = sig * (1.0 + hidden * (1.0 - sig))
        weight = jnp.concatenate([e * ebar for e in envs], axis=1)
        dhidden = slope * (v_col * weight)
        dfeat = dot(linb_s[...], stack_rhs(dhidden))
        ract = jnp.sum(v_col * act, axis=0, keepdims=True)
        for j in range(2):
            k = 2 * p + j
            lanes = slice(j * SITES, (j + 1) * SITES)
            raw = ract[:, lanes] + jnp.sum(r_col * feats[j][:ch], axis=0, keepdims=True)
            scal_s[pl.ds(k, 1), :] = raw
            energy = energy + raw * envs[j]
            df = dfeat[:, lanes]
            d0, d1, d2 = df[ch : 2 * ch], df[2 * ch : 3 * ch], df[3 * ch :]
            dfirst_s[k] = df[:ch] + r_col * weight[:, lanes]
            dgain_s[k] = d0 * s_s[0] + d1 * t1s[j] + d2 * t2s[j]
            dt_s[k] = jnp.concatenate([gains[j] * d0, gains[j] * d1, gains[j] * d2], axis=0)
        return energy

    energy = lax.fori_loop(0, pairs, middle, jnp.zeros((1, SITES), F32))

    for c in range(0, ch, step):

        def gather_ds(k, acc):
            t = [dt_s[k, l * ch + c : l * ch + c + step, :] for l in range(3)]
            out = [acc[0] + t[0]]
            for m in range(1, 9):
                out.append(acc[m] + t[1 if m < 4 else 2] * y_s[k, m : m + 1, :])
            return tuple(out)

        acc = lax.fori_loop(
            0, slots, gather_ds, tuple(jnp.zeros((step, SITES), F32) for _ in range(9)), unroll=4
        )
        for m in range(9):
            ds_s[m, c : c + step, :] = acc[m] * inv_root

    mix3 = stack_lhs(mix_ref[...])
    radial3 = stack_lhs(jnp.concatenate([radial_ref[...], jnp.zeros((8, ch), F32)], axis=0))

    def last(p, carry):
        dmix = []
        for j in range(2):
            k = 2 * p + j
            env = env_s[pl.ds(k, 1), :]
            raw = raw_s[k]
            w = raw * env
            t1 = dt_s[k, ch : 2 * ch, :]
            t2 = dt_s[k, 2 * ch :, :]
            dw = ds_s[0]
            for m in range(1, 9):
                dsm = ds_s[m]
                dw = dw + y_s[k, m : m + 1, :] * dsm
                t = t1 if m < 4 else t2
                dy_s[k, m : m + 1, :] = jnp.sum(t * s_s[m] + w * dsm, axis=0, keepdims=True)
            scal_s[pl.ds(k, 1), :] = scal_s[pl.ds(k, 1), :] * ebar + jnp.sum(
                raw * dw, axis=0, keepdims=True
            )
            dmix.append(jnp.concatenate([dgain_s[k], dw * env], axis=0))
        dfirst = dot(mix3, stack_rhs(jnp.concatenate(dmix, axis=1)))
        dsum = []
        for j in range(2):
            k = 2 * p + j
            dsum.append((dfirst[:, j * SITES : (j + 1) * SITES] + dfirst_s[k]) * sig_s[k])
        dbasis = dot(radial3, stack_rhs(jnp.concatenate(dsum, axis=1)))
        for j in range(2):
            dbasis_s[2 * p + j] = dbasis[:8, j * SITES : (j + 1) * SITES]
        return carry

    lax.fori_loop(0, pairs, last, 0)

    dd = scal_s[...] * denv_dd
    for n in range(radial_ref.shape[0]):
        rate = (n + 1) * math.pi / CUTOFF
        dd = dd + dbasis_s[:, n, :] * ((rate * cosines[n] - sines[n] * inv) * inv)
    y1, y2, y3, y4, y5, y6, y7, y8 = [dy_s[:, m, :] for m in range(1, 9)]
    dux = R3 * y1 + R15 * (uy * y4 + uz * y7 + ux * y8)
    duy = R3 * y2 + R15 * (ux * y4 + uz * y5 - uy * y8)
    duz = R3 * y3 + R15 * (uy * y5 + ux * y7) + 3.0 * R5 * uz * y6
    along = dd - (ux * dux + uy * duy + uz * duz) * inv
    zero = jnp.zeros_like(d)
    own = []
    for n, (u, du) in enumerate(((ux, dux), (uy, duy), (uz, duz))):
        g = u * along + du * inv
        own.append(jnp.sum(g, axis=0, keepdims=True))
        high = g.astype(BF16).astype(F32)
        g_s[:, n, :] = high
        g_s[:, 8 + n, :] = g - high
    for n in range(3, 8):
        g_s[:, n, :] = zero
        g_s[:, 8 + n, :] = zero

    def spread(p, acc):
        g = jnp.concatenate([g_s[2 * p], g_s[2 * p + 1]], axis=1).astype(BF16)
        return acc + lax.dot_general(g, hot_ref[p], NT, preferred_element_type=F32)

    rows = table_ref.shape[1]
    acc = lax.fori_loop(0, pairs, spread, jnp.zeros((16, rows), F32))
    acc = -(acc[:8] + acc[8:])
    own.append(ebar * energy + extra[5:6])
    own.append(jnp.zeros((4, SITES), F32))
    result_ref[0] = acc[:, :SITES] + jnp.concatenate(own, axis=0)
    for t in range(1, rows // SITES):
        result_ref[t] = acc[:, t * SITES : (t + 1) * SITES]


def return_kernel(
    groups, sizes, part_ref, slots_ref, select_ref, out_ref, recv_buf, send_sem, recv_sem
):
    barrier = greet(groups, sizes)
    pl.semaphore_wait(barrier, len(groups))
    copies = []
    for n, (o, (start, _)) in enumerate(groups.items()):
        copies.append(
            pltpu.make_async_remote_copy(
                src_ref=part_ref.at[start // SITES],
                dst_ref=recv_buf.at[n],
                send_sem=send_sem.at[n],
                recv_sem=recv_sem.at[n],
                device_id=device_at(o, sizes),
                device_id_type=pl.DeviceIdType.MESH,
            )
        )
    for copy in copies:
        copy.start()
    for copy in copies:
        copy.wait()
    lane = lax.broadcasted_iota(jnp.int32, (8, SITES), 1)
    total = part_ref[0]
    merged = [jnp.zeros((8, SITES), F32) for _ in range(part_ref.shape[0])]
    for n, (start, sites) in enumerate(groups.values()):
        t, low = start // SITES, start % SITES
        live = (lane >= low) & (lane < low + len(sites))
        merged[t] = merged[t] + jnp.where(live, recv_buf[n], 0.0)
    total = total + exact(
        jnp.concatenate(merged[1:], axis=1), select_ref[...]
    )
    out_ref[...] = lax.dot_general(
        total, slot_site(slots_ref[...]), NT, precision=PRECISE, preferred_element_type=F32
    )


def shards(
    sizes,
    positions,
    attributes,
    species,
    occupied,
    neighbours,
    pair_flags,
    site_slots,
    radial_weight,
    node_weight,
    mix_weight,
    latent_in,
    latent_out,
    readout,
    species_scale,
    species_shift,
):
    groups, select, hot, shift = lattice_plan(sizes[2])
    rows = hot.shape[1]
    slots = shift.shape[1]
    ch = mix_weight.shape[0]
    hid = latent_in.shape[1]
    count = len(groups)
    select = jnp.asarray(select[SITES:])
    hot = jnp.asarray(hot, dtype=BF16)
    site_row = site_slots.reshape(1, SITES)
    own, table = pl.pallas_call(
        functools.partial(ghosts_kernel, groups, sizes, rows),
        out_shape=(
            jax.ShapeDtypeStruct((2 * ch + 8, SITES), F32),
            jax.ShapeDtypeStruct((2 * ch + 32, rows), BF16),
        ),
        in_specs=[SMEM] * 2 + [VMEM] * 7,
        out_specs=(VMEM, VMEM),
        scratch_shapes=[
            pltpu.VMEM((rows - SITES, SITES), F32),
            pltpu.VMEM((rows - SITES, SITES), F32),
            pltpu.SemaphoreType.DMA((count,)),
            pltpu.SemaphoreType.DMA((count,)),
        ],
        compiler_params=pltpu.CompilerParams(
            collective_id=0, has_side_effects=True, vmem_limit_bytes=16 * 2**20
        ),
        name="ghosts",
    )(
        species_scale,
        species_shift,
        positions,
        attributes,
        species.reshape(1, SITES),
        occupied.reshape(1, SITES),
        site_row,
        node_weight,
        select,
    )
    per_slot = lambda *dims: pltpu.VMEM((slots,) + dims + (SITES,), F32)
    parts = pl.pallas_call(
        functools.partial(model_kernel, slots, ch),
        out_shape=jax.ShapeDtypeStruct((rows // SITES, 8, SITES), F32),
        in_specs=[VMEM] * 9,
        out_specs=VMEM,
        scratch_shapes=[
            per_slot(ch),
            per_slot(8),
            per_slot(8),
            per_slot(16),
            per_slot(),
            per_slot(ch),
            per_slot(ch),
            per_slot(ch),
            per_slot(ch),
            pltpu.VMEM((9, ch, SITES), F32),
            pltpu.VMEM((9, ch, SITES), F32),
            per_slot(3 * ch),
            per_slot(ch),
            per_slot(ch),
            per_slot(),
            per_slot(8),
            per_slot(16),
            per_slot(16),
            pltpu.VMEM((hid, 12 * ch), BF16),
            pltpu.VMEM((4 * ch, 3 * hid), BF16),
        ],
        compiler_params=pltpu.CompilerParams(vmem_limit_bytes=40 * 2**20),
        name="model",
    )(
        own,
        table,
        hot,
        jnp.asarray(shift),
        radial_weight,
        mix_weight,
        latent_in,
        latent_out,
        readout.reshape(1, ch),
    )
    out = pl.pallas_call(
        functools.partial(return_kernel, groups, sizes),
        out_shape=jax.ShapeDtypeStruct((8, SITES), F32),
        in_specs=[VMEM] * 3,
        out_specs=VMEM,
        scratch_shapes=[
            pltpu.VMEM((count, 8, SITES), F32),
            pltpu.SemaphoreType.DMA((count,)),
            pltpu.SemaphoreType.DMA((count,)),
        ],
        compiler_params=pltpu.CompilerParams(collective_id=1, has_side_effects=True),
        name="give_back",
    )(parts, site_row, select)
    return (out[3], out[:3])


def solution(mesh):
    sizes = tuple(mesh.shape[a] for a in AXES)
    return jax.shard_map(
        functools.partial(shards, sizes),
        mesh=mesh,
        in_specs=(
            P(None, AXES),
            P(None, AXES),
            P(AXES),
            P(AXES),
            P(None, AXES),
            P(None, AXES),
            P(AXES),
            P(),
            P(),
            P(),
            P(),
            P(),
            P(),
            P(),
            P(),
        ),
        out_specs=(P(AXES), P(None, AXES)),
        check_vma=False,
    )
```

```python
import functools
import math

import jax
import jax.numpy as jnp
import numpy as np
from jax import lax
from jax.experimental import pallas as pl
from jax.experimental.pallas import tpu as pltpu
from jax.sharding import PartitionSpec as P

LXY = 8
LZ = 2
GROUP = 4
SITES = LXY * LXY * LZ
SPACING = 1.5
CUTOFF = 4.0
PRECISE = lax.Precision.HIGHEST
R3 = math.sqrt(3.0)
R5 = math.sqrt(5.0)
R15 = math.sqrt(15.0)
AXES = ("gx", "gy", "gz")
F32 = jnp.float32
BF16 = jnp.bfloat16
NT = (((1,), (1,)), ((), ()))
VMEM = pl.BlockSpec(memory_space=pltpu.VMEM)
ANY = pl.BlockSpec(memory_space=pl.ANY)


def offsets():
    span = range(-2, 3)
    return [
        (dx, dy, dz)
        for dx in span
        for dy in span
        for dz in span
        if 0 < dx * dx + dy * dy + dz * dz <= 4
    ]


def flat(x, y, z):
    return (x * LXY + y) * LZ + z


def lattice_plan(z_bricks):
    z_sides = [1] if z_bricks == 2 else [1, -1]
    groups = {}
    cursor = [SITES]

    def near(side, deep):
        if side == 0:
            return range(LXY)
        if side > 0:
            return range(0, 2 if deep else 1)
        return range(LXY - (2 if deep else 1), LXY)

    def add(o):
        lone = sum(c != 0 for c in o) == 1
        sites = [flat(x, y, z) for x in near(o[0], lone) for y in near(o[1], lone) for z in range(LZ)]
        groups[o] = (cursor[0], sites)
        cursor[0] += -(-len(sites) // 8) * 8

    for o in [(1, 0, 0), (-1, 0, 0), (0, 1, 0), (0, -1, 0)]:
        add(o)
    for oz in z_sides:
        add((0, 0, oz))
    for ox in (1, -1):
        for oy in (1, -1):
            add((ox, oy, 0))
    for oz in z_sides:
        for side in (1, -1):
            add((side, 0, oz))
            add((0, side, oz))
        for ox in (1, -1):
            for oy in (1, -1):
                add((ox, oy, oz))
    rows = -(-cursor[0] // 256) * 256
    select = np.zeros((rows, SITES), np.float32)
    for start, sites in groups.values():
        for n, site in enumerate(sites):
            select[start + n, site] = 1.0
    ds = offsets()
    hot = np.zeros((len(ds), rows, SITES), np.float32)
    shift = np.zeros((3, len(ds), SITES), np.float32)
    edge = (LXY * SPACING, LXY * SPACING, LZ * SPACING)
    for k, d in enumerate(ds):
        for x in range(LXY):
            for y in range(LXY):
                for z in range(LZ):
                    t = (x + d[0], y + d[1], z + d[2])
                    o = (t[0] // LXY, t[1] // LXY, t[2] // LZ)
                    inside = flat(t[0] % LXY, t[1] % LXY, t[2] % LZ)
                    s = flat(x, y, z)
                    for c in range(3):
                        shift[c, k, s] = o[c] * edge[c]
                    if o == (0, 0, 0):
                        g = inside
                    else:
                        key = (o[0], o[1], abs(o[2])) if z_bricks == 2 else o
                        start, sites = groups[key]
                        g = start + sites.index(inside)
                    hot[k, g, s] = 1.0
    hot = hot.reshape(len(ds) // GROUP, GROUP, rows, SITES).transpose(0, 2, 1, 3)
    hot = hot.reshape(len(ds) // GROUP, rows, GROUP * SITES)
    return groups, select, hot, shift


def device_at(o, sizes):
    return tuple(
        lax.rem(lax.axis_index(a) + (c + n), n) if c else lax.axis_index(a)
        for a, c, n in zip(AXES, o, sizes)
    )


def greet(groups, sizes):
    barrier = pltpu.get_barrier_semaphore()
    for o in groups:
        pl.semaphore_signal(
            barrier, inc=1, device_id=device_at(o, sizes), device_id_type=pl.DeviceIdType.MESH
        )
    return barrier


def dot(a, b):
    return jnp.dot(a, b, preferred_element_type=F32)


def exact(a, b):
    return jnp.dot(a, b, precision=PRECISE, preferred_element_type=F32)


def halves(x):
    high = x.astype(BF16)
    return high, (x - high.astype(F32)).astype(BF16)


def stack_rhs(x):
    high, low = halves(x)
    return jnp.concatenate([high, low, high], axis=0)


def stack_lhs(w):
    high = w.astype(BF16).astype(F32)
    return jnp.concatenate([high, high, w - high], axis=1).astype(BF16)


def slot_site(row):
    slot = lax.broadcasted_iota(jnp.int32, (SITES, SITES), 0)
    return jnp.where(slot == row, 1.0, 0.0).astype(F32)


def thirds(x, axis):
    first = x.astype(BF16).astype(F32)
    rest = x - first
    second = rest.astype(BF16).astype(F32)
    return jnp.concatenate([first, second, rest - second], axis=axis).astype(BF16)


def lanes_of(j):
    return slice(j * SITES, (j + 1) * SITES)


def sigmoid(v):
    return 0.5 * jnp.tanh(0.5 * v) + 0.5


def brick_kernel(groups, sizes, rows, slots, ch, names, *refs):
    count = len(names)
    hbm = dict(zip(names, refs[:count]))
    energy_ref, force_ref = refs[count : count + 2]
    local = dict(zip(names, refs[count + 2 : 2 * count + 2]))
    (
        load_sem, send_buf, recv_buf, send_sem, recv_sem, part_s, back_buf, back_send, back_recv,
        table_ref, near_s, q_s, basis_s, y_s, env_s, first_s, sig_s, gain_s, raw_s, s_s,
        ds_s, dt_s, dfirst_s, dgain_s, scal_s, dbasis_s, dy_s, g_s, lin_s, linb_s,
    ) = refs[2 * count + 2 :]
    loads = {
        name: pltpu.make_async_copy(hbm[name], local[name], load_sem.at[n])
        for n, name in enumerate(names)
    }
    for load in loads.values():
        load.start()
    used = max(start + -(-len(sites) // 8) * 8 for start, sites in groups.values())
    if used < rows:
        recv_buf[used - SITES :, :] = jnp.zeros((rows - used, SITES), F32)
    barrier = greet(groups, sizes)
    early = ("node", "attr", "pos", "occ", "species", "scale", "shift", "slots", "select")
    for name in early:
        loads[name].wait()

    terms = dot(stack_lhs(local["node"][...].T), stack_rhs(local["attr"][...]))
    occ = local["occ"][...].astype(F32)
    species = local["species"][...]
    scale = jnp.zeros_like(occ)
    shift = jnp.zeros_like(occ)
    for n in range(hbm["scale"].shape[1]):
        scale = jnp.where(species == n, local["scale"][:, n : n + 1], scale)
        shift = jnp.where(species == n, local["shift"][:, n : n + 1], shift)
    extra = jnp.concatenate(
        [local["pos"][...], occ, occ * scale, occ * shift, jnp.zeros((2, SITES), F32)], axis=0
    )
    data = jnp.concatenate([terms, extra], axis=0)
    hot_sites = slot_site(local["slots"][...]).astype(BF16)
    data = dot(thirds(data, 1), jnp.concatenate([hot_sites] * 3, axis=0))
    sent = jnp.concatenate([data[ch:], jnp.zeros((SITES - ch - 8, SITES), F32)], axis=0)
    select = local["select"][...]
    send_buf[...] = dot(jnp.concatenate([select] * 3, axis=1), thirds(sent.T, 0))
    pl.semaphore_wait(barrier, len(groups))
    copies = []
    for n, (o, (start, sites)) in enumerate(groups.items()):
        back = tuple(-c for c in o)
        part = pl.ds(start - SITES, -(-len(sites) // 8) * 8)
        copies.append(
            pltpu.make_async_remote_copy(
                src_ref=send_buf.at[part],
                dst_ref=recv_buf.at[part],
                send_sem=send_sem.at[n],
                recv_sem=recv_sem.at[n],
                device_id=device_at(back, sizes),
                device_id_type=pl.DeviceIdType.MESH,
            )
        )
    for copy in copies:
        copy.start()

    for name in names:
        if name not in early:
            loads[name].wait()
    radial = local["radial"][...]
    mix = local["mix"][...]
    mix3_t = stack_lhs(mix.T)
    mix3 = stack_lhs(mix)
    lin_s[...] = stack_lhs(local["latent_in"][...].T)
    linb_s[...] = stack_lhs(local["latent_in"][...])
    basis_n = radial.shape[0]
    radial_high = radial.astype(BF16).astype(F32)
    radial_t = jnp.concatenate(
        [radial_high, radial_high, radial - radial_high, jnp.zeros_like(radial)], axis=0
    ).T.astype(BF16)
    radial3 = stack_lhs(jnp.concatenate([radial, jnp.zeros_like(radial)], axis=0))
    readout_row = local["readout"][...]

    def eye(n):
        return lax.broadcasted_iota(jnp.int32, (n, n), 0) == lax.broadcasted_iota(
            jnp.int32, (n, n), 1
        )

    r_col = jnp.sum(jnp.where(eye(ch), readout_row, 0.0), axis=1, keepdims=True)
    v_row = jnp.sum(local["latent_out"][...] * r_col, axis=0, keepdims=True)
    v_col = jnp.sum(jnp.where(eye(v_row.shape[1]), v_row, 0.0), axis=1, keepdims=True)
    shift_ref = local["images"]
    hot_ref = local["hot"]

    def fill(t, near, q):
        near_high = near.astype(BF16).astype(F32)
        q1 = q.astype(BF16).astype(F32)
        q2 = (q - q1).astype(BF16).astype(F32)
        table_ref[:, lanes_of(t)] = jnp.concatenate(
            [near_high, near - near_high, q1, q2, q - q1 - q2, jnp.zeros_like(q)], axis=0
        ).astype(BF16)

    fill(0, data[ch : 2 * ch], data[2 * ch :])
    for copy in copies:
        copy.wait()
    for t in range(1, rows // SITES):
        block = recv_buf[(t - 1) * SITES : t * SITES, :].T
        fill(t, block[:ch], block[ch : ch + 8])

    steps = slots // GROUP
    inv_root = 1.0 / math.sqrt(slots)
    table = table_ref[...]

    def fetch(p, carry):
        got = dot(table, hot_ref[p])
        for j in range(GROUP):
            k = GROUP * p + j
            part = got[:, lanes_of(j)]
            near_s[k] = part[:ch] + part[ch : 2 * ch]
            q = 2 * ch
            q_s[k] = part[q : q + 8] + part[q + 8 : q + 16] + part[q + 16 : q + 24]
        return carry

    lax.fori_loop(0, steps, fetch, 0)

    extra = data[2 * ch :]
    ebar = extra[4:5]
    rx = (q_s[:, 0, :] + shift_ref[0]) - extra[0:1]
    ry = (q_s[:, 1, :] + shift_ref[1]) - extra[1:2]
    rz = (q_s[:, 2, :] + shift_ref[2]) - extra[2:3]
    flag = q_s[:, 3, :] * extra[3:4]
    d = jnp.sqrt(rx * rx + ry * ry + rz * rz)
    inv = 1.0 / d
    ux, uy, uz = rx * inv, ry * inv, rz * inv
    y_s[:, 0, :] = jnp.ones_like(ux)
    y_s[:, 1, :] = R3 * ux
    y_s[:, 2, :] = R3 * uy
    y_s[:, 3, :] = R3 * uz
    y_s[:, 4, :] = R15 * ux * uy
    y_s[:, 5, :] = R15 * uy * uz
    y_s[:, 6, :] = 0.5 * R5 * (3.0 * uz * uz - 1.0)
    y_s[:, 7, :] = R15 * ux * uz
    y_s[:, 8, :] = 0.5 * R15 * (ux * ux - uy * uy)
    scaled = d * (1.0 / CUTOFF)
    base = 1.0 - scaled * scaled
    env_s[...] = base * base * flag
    denv_dd = base * scaled * flag * (-4.0 / CUTOFF)
    angle = d * (math.pi / CUTOFF)
    sines = [jnp.sin(angle)]
    cosines = [jnp.cos(angle)]
    for n in range(1, basis_n):
        sines.append(sines[0] * cosines[-1] + cosines[0] * sines[-1])
        cosines.append(cosines[0] * cosines[-1] - sines[0] * sines[n - 1])
    for n in range(basis_n):
        basis_s[:, n, :] = sines[n] * inv

    centre = data[:ch]

    def first(p, carry):
        basis = jnp.concatenate([basis_s[GROUP * p + j] for j in range(GROUP)], axis=1)
        high = basis.astype(BF16).astype(F32)
        basis = jnp.concatenate([high, basis - high, high, jnp.zeros_like(high)], axis=0)
        radial = dot(radial_t, basis.astype(BF16))
        total = []
        for j in range(GROUP):
            k = GROUP * p + j
            v = radial[:, lanes_of(j)] + centre + near_s[k]
            sig = sigmoid(v)
            act = v * sig
            first_s[k] = act
            sig_s[k] = sig * (1.0 + v * (1.0 - sig))
            total.append(act)
        mixture = dot(mix3_t, stack_rhs(jnp.concatenate(total, axis=1)))
        for j in range(GROUP):
            k = GROUP * p + j
            part = mixture[:, lanes_of(j)]
            gain_s[k] = part[:ch]
            raw_s[k] = part[ch:]
        return carry

    lax.fori_loop(0, steps, first, 0)

    step = 16
    for c in range(0, ch, step):

        def gather_s(k, acc):
            w = raw_s[k, c : c + step, :] * env_s[pl.ds(k, 1), :]
            return tuple(a + w * (y_s[k, m : m + 1, :]) if m else a + w for m, a in enumerate(acc))

        acc = lax.fori_loop(
            0, slots, gather_s, tuple(jnp.zeros((step, SITES), F32) for _ in range(9)), unroll=4
        )
        for m in range(9):
            s_s[m, c : c + step, :] = acc[m] * inv_root

    def middle(p, energy):
        feats, gains, t1s, t2s, envs = [], [], [], [], []
        for j in range(GROUP):
            k = GROUP * p + j
            y = [y_s[k, m : m + 1, :] for m in range(9)]
            t1 = y[1] * s_s[1]
            for m in (2, 3):
                t1 = t1 + y[m] * s_s[m]
            t2 = y[4] * s_s[4]
            for m in (5, 6, 7, 8):
                t2 = t2 + y[m] * s_s[m]
            gain = gain_s[k]
            feats.append(jnp.concatenate([first_s[k], gain * s_s[0], gain * t1, gain * t2], axis=0))
            gains.append(gain)
            t1s.append(t1)
            t2s.append(t2)
            envs.append(env_s[pl.ds(k, 1), :])
        hidden = dot(lin_s[...], stack_rhs(jnp.concatenate(feats, axis=1)))
        sig = sigmoid(hidden)
        act = hidden * sig
        slope = sig * (1.0 + hidden * (1.0 - sig))
        weight = jnp.concatenate([e * ebar for e in envs], axis=1)
        dhidden = slope * (v_col * weight)
        dfeat = dot(linb_s[...], stack_rhs(dhidden))
        ract = jnp.sum(v_col * act, axis=0, keepdims=True)
        for j in range(GROUP):
            k = GROUP * p + j
            lanes = lanes_of(j)
            raw = ract[:, lanes] + jnp.sum(r_col * feats[j][:ch], axis=0, keepdims=True)
            scal_s[pl.ds(k, 1), :] = raw
            energy = energy + raw * envs[j]
            df = dfeat[:, lanes]
            d0, d1, d2 = df[ch : 2 * ch], df[2 * ch : 3 * ch], df[3 * ch :]
            dfirst_s[k] = df[:ch] + r_col * weight[:, lanes]
            dgain_s[k] = d0 * s_s[0] + d1 * t1s[j] + d2 * t2s[j]
            dt_s[k] = jnp.concatenate([gains[j] * d0, gains[j] * d1, gains[j] * d2], axis=0)
        return energy

    energy = lax.fori_loop(0, steps, middle, jnp.zeros((1, SITES), F32))

    for c in range(0, ch, step):

        def gather_ds(k, acc):
            t = [dt_s[k, l * ch + c : l * ch + c + step, :] for l in range(3)]
            out = [acc[0] + t[0]]
            for m in range(1, 9):
                out.append(acc[m] + t[1 if m < 4 else 2] * y_s[k, m : m + 1, :])
            return tuple(out)

        acc = lax.fori_loop(
            0, slots, gather_ds, tuple(jnp.zeros((step, SITES), F32) for _ in range(9)), unroll=4
        )
        for m in range(9):
            ds_s[m, c : c + step, :] = acc[m] * inv_root

    def last(p, carry):
        dmix = []
        for j in range(GROUP):
            k = GROUP * p + j
            env = env_s[pl.ds(k, 1), :]
            raw = raw_s[k]
            w = raw * env
            t1 = dt_s[k, ch : 2 * ch, :]
            t2 = dt_s[k, 2 * ch :, :]
            dw = ds_s[0]
            for m in range(1, 9):
                dsm = ds_s[m]
                dw = dw + y_s[k, m : m + 1, :] * dsm
                t = t1 if m < 4 else t2
                dy_s[k, m : m + 1, :] = jnp.sum(t * s_s[m] + w * dsm, axis=0, keepdims=True)
            scal_s[pl.ds(k, 1), :] = scal_s[pl.ds(k, 1), :] * ebar + jnp.sum(
                raw * dw, axis=0, keepdims=True
            )
            dmix.append(jnp.concatenate([dgain_s[k], dw * env], axis=0))
        dfirst = dot(mix3, stack_rhs(jnp.concatenate(dmix, axis=1)))
        dsum = []
        for j in range(GROUP):
            k = GROUP * p + j
            dsum.append((dfirst[:, lanes_of(j)] + dfirst_s[k]) * sig_s[k])
        dbasis = dot(radial3, stack_rhs(jnp.concatenate(dsum, axis=1)))
        for j in range(GROUP):
            dbasis_s[GROUP * p + j] = dbasis[:8, lanes_of(j)]
        return carry

    lax.fori_loop(0, steps, last, 0)

    dd = scal_s[...] * denv_dd
    for n in range(basis_n):
        rate = (n + 1) * math.pi / CUTOFF
        dd = dd + dbasis_s[:, n, :] * ((rate * cosines[n] - sines[n] * inv) * inv)
    y1, y2, y3, y4, y5, y6, y7, y8 = [dy_s[:, m, :] for m in range(1, 9)]
    dux = R3 * y1 + R15 * (uy * y4 + uz * y7 + ux * y8)
    duy = R3 * y2 + R15 * (ux * y4 + uz * y5 - uy * y8)
    duz = R3 * y3 + R15 * (uy * y5 + ux * y7) + 3.0 * R5 * uz * y6
    along = dd - (ux * dux + uy * duy + uz * duz) * inv
    zero = jnp.zeros_like(d)
    own = []
    for n, (u, du) in enumerate(((ux, dux), (uy, duy), (uz, duz))):
        g = u * along + du * inv
        own.append(jnp.sum(g, axis=0, keepdims=True))
        high = g.astype(BF16).astype(F32)
        g_s[:, n, :] = high
        g_s[:, 8 + n, :] = g - high
    for n in range(3, 8):
        g_s[:, n, :] = zero
        g_s[:, 8 + n, :] = zero

    def spread(p, acc):
        g = jnp.concatenate([g_s[GROUP * p + j] for j in range(GROUP)], axis=1).astype(BF16)
        return acc + lax.dot_general(g, hot_ref[p], NT, preferred_element_type=F32)

    acc = lax.fori_loop(0, steps, spread, jnp.zeros((16, rows), F32))
    acc = -(acc[:8] + acc[8:])
    own.append(ebar * energy + extra[5:6])
    own.append(jnp.zeros((4, SITES), F32))
    part_s[0] = acc[:, :SITES] + jnp.concatenate(own, axis=0)
    for t in range(1, rows // SITES):
        part_s[t] = acc[:, lanes_of(t)]
    copies = []
    for n, (o, (start, _)) in enumerate(groups.items()):
        copies.append(
            pltpu.make_async_remote_copy(
                src_ref=part_s.at[start // SITES],
                dst_ref=back_buf.at[n],
                send_sem=back_send.at[n],
                recv_sem=back_recv.at[n],
                device_id=device_at(o, sizes),
                device_id_type=pl.DeviceIdType.MESH,
            )
        )
    for copy in copies:
        copy.start()
    for copy in copies:
        copy.wait()
    lane = lax.broadcasted_iota(jnp.int32, (8, SITES), 1)
    merged = [jnp.zeros((8, SITES), F32) for _ in range(rows // SITES)]
    for n, (start, sites) in enumerate(groups.values()):
        t, low = start // SITES, start % SITES
        live = (lane >= low) & (lane < low + len(sites))
        merged[t] = merged[t] + jnp.where(live, back_buf[n], 0.0)
    select3 = jnp.concatenate([local["select"][...]] * 3, axis=0)
    total = part_s[0] + dot(thirds(jnp.concatenate(merged[1:], axis=1), 1), select3)
    hot3 = jnp.concatenate([slot_site(local["slots"][...]).astype(BF16)] * 3, axis=1)
    out = lax.dot_general(thirds(total, 1), hot3, NT, preferred_element_type=F32)
    energy_ref[...] = out[3:4]
    force_ref[...] = out[:3]


def shards(
    sizes,
    positions,
    attributes,
    species,
    occupied,
    neighbours,
    pair_flags,
    site_slots,
    radial_weight,
    node_weight,
    mix_weight,
    latent_in,
    latent_out,
    readout,
    species_scale,
    species_shift,
):
    groups, select, hot, images = lattice_plan(sizes[2])
    rows = hot.shape[1]
    slots = images.shape[1]
    ch = mix_weight.shape[0]
    hid = latent_in.shape[1]
    count = len(groups)
    operands = {
        "node": node_weight,
        "attr": attributes,
        "pos": positions,
        "occ": occupied.reshape(1, SITES),
        "species": species.reshape(1, SITES),
        "scale": species_scale.reshape(1, -1),
        "shift": species_shift.reshape(1, -1),
        "slots": site_slots.reshape(1, SITES),
        "select": jnp.asarray(select[SITES:], dtype=BF16),
        "hot": jnp.asarray(hot, dtype=BF16),
        "images": jnp.asarray(images),
        "radial": radial_weight,
        "mix": mix_weight,
        "latent_in": latent_in,
        "latent_out": latent_out.T,
        "readout": readout.reshape(1, ch),
    }
    names = tuple(operands)
    dma = pltpu.SemaphoreType.DMA
    per_slot = lambda *dims: pltpu.VMEM((slots,) + dims + (SITES,), F32)
    energy, forces = pl.pallas_call(
        functools.partial(brick_kernel, groups, sizes, rows, slots, ch, names),
        out_shape=(
            jax.ShapeDtypeStruct((1, SITES), F32),
            jax.ShapeDtypeStruct((3, SITES), F32),
        ),
        in_specs=[ANY] * len(names),
        out_specs=(VMEM, VMEM),
        scratch_shapes=[pltpu.VMEM(v.shape, v.dtype) for v in operands.values()]
        + [
            dma((len(names),)),
            pltpu.VMEM((rows - SITES, SITES), F32),
            pltpu.VMEM((rows - SITES, SITES), F32),
            dma((count,)),
            dma((count,)),
            pltpu.VMEM((rows // SITES, 8, SITES), F32),
            pltpu.VMEM((count, 8, SITES), F32),
            dma((count,)),
            dma((count,)),
            pltpu.VMEM((2 * ch + 32, rows), BF16),
            per_slot(ch),
            per_slot(8),
            per_slot(8),
            per_slot(16),
            per_slot(),
            per_slot(ch),
            per_slot(ch),
            per_slot(ch),
            per_slot(ch),
            pltpu.VMEM((9, ch, SITES), F32),
            pltpu.VMEM((9, ch, SITES), F32),
            per_slot(3 * ch),
            per_slot(ch),
            per_slot(ch),
            per_slot(),
            per_slot(8),
            per_slot(16),
            per_slot(16),
            pltpu.VMEM((hid, 12 * ch), BF16),
            pltpu.VMEM((4 * ch, 3 * hid), BF16),
        ],
        compiler_params=pltpu.CompilerParams(
            collective_id=0, has_side_effects=True, vmem_limit_bytes=56 * 2**20
        ),
        name="brick",
    )(*operands.values())
    return (energy.reshape(SITES), forces)


def solution(mesh):
    sizes = tuple(mesh.shape[a] for a in AXES)
    return jax.shard_map(
        functools.partial(shards, sizes),
        mesh=mesh,
        in_specs=(
            P(None, AXES),
            P(None, AXES),
            P(AXES),
            P(AXES),
            P(None, AXES),
            P(None, AXES),
            P(AXES),
            P(),
            P(),
            P(),
            P(),
            P(),
            P(),
            P(),
            P(),
        ),
        out_specs=(P(AXES), P(None, AXES)),
        check_vma=False,
    )
```

```python
import functools
import math

import jax
import jax.numpy as jnp
import numpy as np
from jax import lax
from jax.experimental import pallas as pl
from jax.experimental.pallas import tpu as pltpu
from jax.sharding import PartitionSpec as P

LXY = 8
LZ = 2
GROUP = 16
SITES = LXY * LXY * LZ
SPACING = 1.5
CUTOFF = 4.0
PRECISE = lax.Precision.HIGHEST
R3 = math.sqrt(3.0)
R5 = math.sqrt(5.0)
R15 = math.sqrt(15.0)
AXES = ("gx", "gy", "gz")
F32 = jnp.float32
BF16 = jnp.bfloat16
NT = (((1,), (1,)), ((), ()))
VMEM = pl.BlockSpec(memory_space=pltpu.VMEM)
ANY = pl.BlockSpec(memory_space=pl.ANY)


def offsets():
    span = range(-2, 3)
    return [
        (dx, dy, dz)
        for dx in span
        for dy in span
        for dz in span
        if 0 < dx * dx + dy * dy + dz * dz <= 4
    ]


def flat(x, y, z):
    return (x * LXY + y) * LZ + z


def lattice_plan(z_bricks):
    z_sides = [1] if z_bricks == 2 else [1, -1]
    groups = {}
    cursor = [SITES]

    def near(side, deep):
        if side == 0:
            return range(LXY)
        if side > 0:
            return range(0, 2 if deep else 1)
        return range(LXY - (2 if deep else 1), LXY)

    def add(o):
        lone = sum(c != 0 for c in o) == 1
        sites = [flat(x, y, z) for x in near(o[0], lone) for y in near(o[1], lone) for z in range(LZ)]
        groups[o] = (cursor[0], sites)
        cursor[0] += -(-len(sites) // 8) * 8

    for o in [(1, 0, 0), (-1, 0, 0), (0, 1, 0), (0, -1, 0)]:
        add(o)
    for oz in z_sides:
        add((0, 0, oz))
    for ox in (1, -1):
        for oy in (1, -1):
            add((ox, oy, 0))
    for oz in z_sides:
        for side in (1, -1):
            add((side, 0, oz))
            add((0, side, oz))
        for ox in (1, -1):
            for oy in (1, -1):
                add((ox, oy, oz))
    rows = -(-cursor[0] // 256) * 256
    select = np.zeros((rows, SITES), np.float32)
    for start, sites in groups.values():
        for n, site in enumerate(sites):
            select[start + n, site] = 1.0
    ds = offsets()
    hot = np.zeros((len(ds), rows, SITES), np.float32)
    shift = np.zeros((3, len(ds), SITES), np.float32)
    edge = (LXY * SPACING, LXY * SPACING, LZ * SPACING)
    for k, d in enumerate(ds):
        for x in range(LXY):
            for y in range(LXY):
                for z in range(LZ):
                    t = (x + d[0], y + d[1], z + d[2])
                    o = (t[0] // LXY, t[1] // LXY, t[2] // LZ)
                    inside = flat(t[0] % LXY, t[1] % LXY, t[2] % LZ)
                    s = flat(x, y, z)
                    for c in range(3):
                        shift[c, k, s] = o[c] * edge[c]
                    if o == (0, 0, 0):
                        g = inside
                    else:
                        key = (o[0], o[1], abs(o[2])) if z_bricks == 2 else o
                        start, sites = groups[key]
                        g = start + sites.index(inside)
                    hot[k, g, s] = 1.0
    hot = hot.reshape(len(ds) // GROUP, GROUP, rows, SITES).transpose(0, 2, 1, 3)
    hot = hot.reshape(len(ds) // GROUP, rows, GROUP * SITES)
    return groups, select, hot, shift


def whole_face(o):
    return o[:2] == (0, 0)


def device_at(o, sizes):
    return tuple(
        lax.rem(lax.axis_index(a) + (c + n), n) if c else lax.axis_index(a)
        for a, c, n in zip(AXES, o, sizes)
    )


def greet(groups, sizes):
    barrier = pltpu.get_barrier_semaphore()
    for o in groups:
        pl.semaphore_signal(
            barrier, inc=1, device_id=device_at(o, sizes), device_id_type=pl.DeviceIdType.MESH
        )
    return barrier


def dot(a, b):
    return jnp.dot(a, b, preferred_element_type=F32)


def exact(a, b):
    return jnp.dot(a, b, precision=PRECISE, preferred_element_type=F32)


def halves(x):
    high = x.astype(BF16)
    return high, (x - high.astype(F32)).astype(BF16)


def stack_rhs(x):
    high, low = halves(x)
    return jnp.concatenate([high, low, high], axis=0)


def stack_lhs(w):
    high = w.astype(BF16).astype(F32)
    return jnp.concatenate([high, high, w - high], axis=1).astype(BF16)


def slot_site(row):
    slot = lax.broadcasted_iota(jnp.int32, (SITES, SITES), 0)
    return jnp.where(slot == row, 1.0, 0.0).astype(F32)


def thirds(x, axis):
    first = x.astype(BF16).astype(F32)
    rest = x - first
    second = rest.astype(BF16).astype(F32)
    return jnp.concatenate([first, second, rest - second], axis=axis).astype(BF16)


def lanes_of(j):
    return slice(j * SITES, (j + 1) * SITES)


def sigmoid(v):
    return 0.5 * jnp.tanh(0.5 * v) + 0.5


def brick_kernel(groups, sizes, rows, slots, ch, names, *refs):
    count = len(names)
    hbm = dict(zip(names, refs[:count]))
    energy_ref, force_ref = refs[count : count + 2]
    local = dict(zip(names, refs[count + 2 : 2 * count + 2]))
    (
        load_sem, face_out, face_in, send_buf, recv_buf, send_sem, recv_sem, part_s, back_buf, back_send, back_recv,
        table_ref, near_s, q_s, basis_s, y_s, env_s, first_s, sig_s, gain_s, raw_s, s_s,
        ds_s, dt_s, dfirst_s, dgain_s, scal_s, dbasis_s, dy_s, g_s, lin_s, linb_s,
    ) = refs[2 * count + 2 :]
    loads = {
        name: pltpu.make_async_copy(hbm[name], local[name], load_sem.at[n])
        for n, name in enumerate(names)
    }
    for load in loads.values():
        load.start()
    used = max(start + -(-len(sites) // 8) * 8 for start, sites in groups.values())
    if used < rows:
        recv_buf[used - SITES :, :] = jnp.zeros((rows - used, SITES), F32)
    barrier = greet(groups, sizes)
    early = ("node", "attr", "pos", "occ", "species", "scale", "shift", "slots", "select")
    for name in early:
        loads[name].wait()

    terms = dot(stack_lhs(local["node"][...].T), stack_rhs(local["attr"][...]))
    occ = local["occ"][...].astype(F32)
    species = local["species"][...]
    scale = jnp.zeros_like(occ)
    shift = jnp.zeros_like(occ)
    for n in range(hbm["scale"].shape[1]):
        scale = jnp.where(species == n, local["scale"][:, n : n + 1], scale)
        shift = jnp.where(species == n, local["shift"][:, n : n + 1], shift)
    extra = jnp.concatenate(
        [local["pos"][...], occ, occ * scale, occ * shift, jnp.zeros((2, SITES), F32)], axis=0
    )
    data = jnp.concatenate([terms, extra], axis=0)
    hot_sites = slot_site(local["slots"][...]).astype(BF16)
    data = dot(thirds(data, 1), jnp.concatenate([hot_sites] * 3, axis=0))
    face_out[...] = data[ch:]
    sent = jnp.concatenate([data[ch:], jnp.zeros((SITES - ch - 8, SITES), F32)], axis=0)
    select = local["select"][...]
    send_buf[...] = dot(jnp.concatenate([select] * 3, axis=1), thirds(sent.T, 0))
    pl.semaphore_wait(barrier, len(groups))
    copies = []
    face_tiles = []
    for n, (o, (start, sites)) in enumerate(sorted(groups.items(), key=lambda v: not whole_face(v[0]))):
        back = tuple(-c for c in o)
        part = pl.ds(start - SITES, -(-len(sites) // 8) * 8)
        source, target = send_buf.at[part], recv_buf.at[part]
        if whole_face(o):
            source, target = face_out, face_in.at[len(face_tiles)]
            face_tiles.append(start // SITES)
        copies.append(
            pltpu.make_async_remote_copy(
                src_ref=source,
                dst_ref=target,
                send_sem=send_sem.at[n],
                recv_sem=recv_sem.at[n],
                device_id=device_at(back, sizes),
                device_id_type=pl.DeviceIdType.MESH,
            )
        )
    for copy in copies:
        copy.start()

    for name in names:
        if name not in early:
            loads[name].wait()
    radial = local["radial"][...]
    mix = local["mix"][...]
    mix3_t = stack_lhs(mix.T)
    mix3 = stack_lhs(mix)
    lin_s[...] = stack_lhs(local["latent_in"][...].T)
    linb_s[...] = stack_lhs(local["latent_in"][...])
    basis_n = radial.shape[0]
    radial_high = radial.astype(BF16).astype(F32)
    radial_t = jnp.concatenate(
        [radial_high, radial_high, radial - radial_high, jnp.zeros_like(radial)], axis=0
    ).T.astype(BF16)
    radial3 = stack_lhs(jnp.concatenate([radial, jnp.zeros_like(radial)], axis=0))
    readout_row = local["readout"][...]

    def eye(n):
        return lax.broadcasted_iota(jnp.int32, (n, n), 0) == lax.broadcasted_iota(
            jnp.int32, (n, n), 1
        )

    r_col = jnp.sum(jnp.where(eye(ch), readout_row, 0.0), axis=1, keepdims=True)
    v_row = jnp.sum(local["latent_out"][...] * r_col, axis=0, keepdims=True)
    v_col = jnp.sum(jnp.where(eye(v_row.shape[1]), v_row, 0.0), axis=1, keepdims=True)
    shift_ref = local["images"]
    hot_ref = local["hot"]

    def fill(t, near, q):
        near_high = near.astype(BF16).astype(F32)
        q1 = q.astype(BF16).astype(F32)
        q2 = (q - q1).astype(BF16).astype(F32)
        table_ref[:, lanes_of(t)] = jnp.concatenate(
            [near_high, near - near_high, q1, q2, q - q1 - q2, jnp.zeros_like(q)], axis=0
        ).astype(BF16)

    fill(0, data[ch : 2 * ch], data[2 * ch :])
    for copy in copies:
        copy.wait()
    for t in range(1, rows // SITES):
        if t in face_tiles:
            block = face_in[face_tiles.index(t)]
        else:
            block = recv_buf[(t - 1) * SITES : t * SITES, :].T
        fill(t, block[:ch], block[ch : ch + 8])

    steps = slots // GROUP
    inv_root = 1.0 / math.sqrt(slots)
    table = table_ref[...]

    def fetch(p, carry):
        got = dot(table, hot_ref[p])
        for j in range(GROUP):
            k = GROUP * p + j
            part = got[:, lanes_of(j)]
            near_s[k] = part[:ch] + part[ch : 2 * ch]
            q = 2 * ch
            q_s[k] = part[q : q + 8] + part[q + 8 : q + 16] + part[q + 16 : q + 24]
        return carry

    lax.fori_loop(0, steps, fetch, 0)

    extra = data[2 * ch :]
    ebar = extra[4:5]
    rx = (q_s[:, 0, :] + shift_ref[0]) - extra[0:1]
    ry = (q_s[:, 1, :] + shift_ref[1]) - extra[1:2]
    rz = (q_s[:, 2, :] + shift_ref[2]) - extra[2:3]
    flag = q_s[:, 3, :] * extra[3:4]
    d = jnp.sqrt(rx * rx + ry * ry + rz * rz)
    inv = 1.0 / d
    ux, uy, uz = rx * inv, ry * inv, rz * inv
    y_s[:, 0, :] = jnp.ones_like(ux)
    y_s[:, 1, :] = R3 * ux
    y_s[:, 2, :] = R3 * uy
    y_s[:, 3, :] = R3 * uz
    y_s[:, 4, :] = R15 * ux * uy
    y_s[:, 5, :] = R15 * uy * uz
    y_s[:, 6, :] = 0.5 * R5 * (3.0 * uz * uz - 1.0)
    y_s[:, 7, :] = R15 * ux * uz
    y_s[:, 8, :] = 0.5 * R15 * (ux * ux - uy * uy)
    scaled = d * (1.0 / CUTOFF)
    base = 1.0 - scaled * scaled
    env_s[...] = base * base * flag
    denv_dd = base * scaled * flag * (-4.0 / CUTOFF)
    angle = d * (math.pi / CUTOFF)
    sines = [jnp.sin(angle)]
    cosines = [jnp.cos(angle)]
    for n in range(1, basis_n):
        sines.append(sines[0] * cosines[-1] + cosines[0] * sines[-1])
        cosines.append(cosines[0] * cosines[-1] - sines[0] * sines[n - 1])
    for n in range(basis_n):
        basis_s[:, n, :] = sines[n] * inv

    centre = data[:ch]

    def first(p, carry):
        basis = jnp.concatenate([basis_s[GROUP * p + j] for j in range(GROUP)], axis=1)
        high = basis.astype(BF16).astype(F32)
        basis = jnp.concatenate([high, basis - high, high, jnp.zeros_like(high)], axis=0)
        radial = dot(radial_t, basis.astype(BF16))
        total = []
        for j in range(GROUP):
            k = GROUP * p + j
            v = radial[:, lanes_of(j)] + centre + near_s[k]
            sig = sigmoid(v)
            act = v * sig
            first_s[k] = act
            sig_s[k] = sig * (1.0 + v * (1.0 - sig))
            total.append(act)
        mixture = dot(mix3_t, stack_rhs(jnp.concatenate(total, axis=1)))
        for j in range(GROUP):
            k = GROUP * p + j
            part = mixture[:, lanes_of(j)]
            gain_s[k] = part[:ch]
            raw_s[k] = part[ch:]
        return carry

    lax.fori_loop(0, steps, first, 0)

    step = 16
    for c in range(0, ch, step):

        def gather_s(k, acc):
            w = raw_s[k, c : c + step, :] * env_s[pl.ds(k, 1), :]
            return tuple(a + w * (y_s[k, m : m + 1, :]) if m else a + w for m, a in enumerate(acc))

        acc = lax.fori_loop(
            0, slots, gather_s, tuple(jnp.zeros((step, SITES), F32) for _ in range(9)), unroll=4
        )
        for m in range(9):
            s_s[m, c : c + step, :] = acc[m] * inv_root

    def middle(p, energy):
        feats, gains, t1s, t2s, envs = [], [], [], [], []
        for j in range(GROUP):
            k = GROUP * p + j
            y = [y_s[k, m : m + 1, :] for m in range(9)]
            t1 = y[1] * s_s[1]
            for m in (2, 3):
                t1 = t1 + y[m] * s_s[m]
            t2 = y[4] * s_s[4]
            for m in (5, 6, 7, 8):
                t2 = t2 + y[m] * s_s[m]
            gain = gain_s[k]
            feats.append(jnp.concatenate([first_s[k], gain * s_s[0], gain * t1, gain * t2], axis=0))
            gains.append(gain)
            t1s.append(t1)
            t2s.append(t2)
            envs.append(env_s[pl.ds(k, 1), :])
        hidden = dot(lin_s[...], stack_rhs(jnp.concatenate(feats, axis=1)))
        sig = sigmoid(hidden)
        act = hidden * sig
        slope = sig * (1.0 + hidden * (1.0 - sig))
        weight = jnp.concatenate([e * ebar for e in envs], axis=1)
        dhidden = slope * (v_col * weight)
        dfeat = dot(linb_s[...], stack_rhs(dhidden))
        ract = jnp.sum(v_col * act, axis=0, keepdims=True)
        for j in range(GROUP):
            k = GROUP * p + j
            lanes = lanes_of(j)
            raw = ract[:, lanes] + jnp.sum(r_col * feats[j][:ch], axis=0, keepdims=True)
            scal_s[pl.ds(k, 1), :] = raw
            energy = energy + raw * envs[j]
            df = dfeat[:, lanes]
            d0, d1, d2 = df[ch : 2 * ch], df[2 * ch : 3 * ch], df[3 * ch :]
            dfirst_s[k] = df[:ch] + r_col * weight[:, lanes]
            dgain_s[k] = d0 * s_s[0] + d1 * t1s[j] + d2 * t2s[j]
            dt_s[k] = jnp.concatenate([gains[j] * d0, gains[j] * d1, gains[j] * d2], axis=0)
        return energy

    energy = lax.fori_loop(0, steps, middle, jnp.zeros((1, SITES), F32))

    for c in range(0, ch, step):

        def gather_ds(k, acc):
            t = [dt_s[k, l * ch + c : l * ch + c + step, :] for l in range(3)]
            out = [acc[0] + t[0]]
            for m in range(1, 9):
                out.append(acc[m] + t[1 if m < 4 else 2] * y_s[k, m : m + 1, :])
            return tuple(out)

        acc = lax.fori_loop(
            0, slots, gather_ds, tuple(jnp.zeros((step, SITES), F32) for _ in range(9)), unroll=4
        )
        for m in range(9):
            ds_s[m, c : c + step, :] = acc[m] * inv_root

    def last(p, carry):
        dmix = []
        for j in range(GROUP):
            k = GROUP * p + j
            env = env_s[pl.ds(k, 1), :]
            raw = raw_s[k]
            w = raw * env
            t1 = dt_s[k, ch : 2 * ch, :]
            t2 = dt_s[k, 2 * ch :, :]
            dw = ds_s[0]
            for m in range(1, 9):
                dsm = ds_s[m]
                dw = dw + y_s[k, m : m + 1, :] * dsm
                t = t1 if m < 4 else t2
                dy_s[k, m : m + 1, :] = jnp.sum(t * s_s[m] + w * dsm, axis=0, keepdims=True)
            scal_s[pl.ds(k, 1), :] = scal_s[pl.ds(k, 1), :] * ebar + jnp.sum(
                raw * dw, axis=0, keepdims=True
            )
            dmix.append(jnp.concatenate([dgain_s[k], dw * env], axis=0))
        dfirst = dot(mix3, stack_rhs(jnp.concatenate(dmix, axis=1)))
        dsum = []
        for j in range(GROUP):
            k = GROUP * p + j
            dsum.append((dfirst[:, lanes_of(j)] + dfirst_s[k]) * sig_s[k])
        dbasis = dot(radial3, stack_rhs(jnp.concatenate(dsum, axis=1)))
        for j in range(GROUP):
            dbasis_s[GROUP * p + j] = dbasis[:8, lanes_of(j)]
        return carry

    lax.fori_loop(0, steps, last, 0)

    dd = scal_s[...] * denv_dd
    for n in range(basis_n):
        rate = (n + 1) * math.pi / CUTOFF
        dd = dd + dbasis_s[:, n, :] * ((rate * cosines[n] - sines[n] * inv) * inv)
    y1, y2, y3, y4, y5, y6, y7, y8 = [dy_s[:, m, :] for m in range(1, 9)]
    dux = R3 * y1 + R15 * (uy * y4 + uz * y7 + ux * y8)
    duy = R3 * y2 + R15 * (ux * y4 + uz * y5 - uy * y8)
    duz = R3 * y3 + R15 * (uy * y5 + ux * y7) + 3.0 * R5 * uz * y6
    along = dd - (ux * dux + uy * duy + uz * duz) * inv
    zero = jnp.zeros_like(d)
    own = []
    for n, (u, du) in enumerate(((ux, dux), (uy, duy), (uz, duz))):
        g = u * along + du * inv
        own.append(jnp.sum(g, axis=0, keepdims=True))
        high = g.astype(BF16).astype(F32)
        g_s[:, n, :] = high
        g_s[:, 8 + n, :] = g - high
    for n in range(3, 8):
        g_s[:, n, :] = zero
        g_s[:, 8 + n, :] = zero

    def spread(first_row, size):
        def add(p, acc):
            g = jnp.concatenate([g_s[GROUP * p + j] for j in range(GROUP)], axis=1).astype(BF16)
            hot = hot_ref[p, first_row : first_row + size, :]
            return acc + lax.dot_general(g, hot, NT, preferred_element_type=F32)

        acc = lax.fori_loop(0, steps, add, jnp.zeros((16, size), F32), unroll=True)
        return -(acc[:8] + acc[8:])

    acc = spread(SITES, rows - SITES)
    for t in range(1, rows // SITES):
        part_s[t] = acc[:, lanes_of(t - 1)]
    copies = []
    for n, (o, (start, _)) in enumerate(groups.items()):
        copies.append(
            pltpu.make_async_remote_copy(
                src_ref=part_s.at[start // SITES],
                dst_ref=back_buf.at[n],
                send_sem=back_send.at[n],
                recv_sem=back_recv.at[n],
                device_id=device_at(o, sizes),
                device_id_type=pl.DeviceIdType.MESH,
            )
        )
    for copy in copies:
        copy.start()
    own.append(ebar * energy + extra[5:6])
    own.append(jnp.zeros((4, SITES), F32))
    total = spread(0, SITES) + jnp.concatenate(own, axis=0)
    for copy in copies:
        copy.wait()
    lane = lax.broadcasted_iota(jnp.int32, (8, SITES), 1)
    merged = [jnp.zeros((8, SITES), F32) for _ in range(rows // SITES)]
    for n, (start, sites) in enumerate(groups.values()):
        t, low = start // SITES, start % SITES
        live = (lane >= low) & (lane < low + len(sites))
        merged[t] = merged[t] + jnp.where(live, back_buf[n], 0.0)
    select3 = jnp.concatenate([local["select"][...]] * 3, axis=0)
    total = total + dot(thirds(jnp.concatenate(merged[1:], axis=1), 1), select3)
    hot3 = jnp.concatenate([slot_site(local["slots"][...]).astype(BF16)] * 3, axis=1)
    out = lax.dot_general(thirds(total, 1), hot3, NT, preferred_element_type=F32)
    energy_ref[...] = out[3:4]
    force_ref[...] = out[:3]


def shards(
    sizes,
    positions,
    attributes,
    species,
    occupied,
    neighbours,
    pair_flags,
    site_slots,
    radial_weight,
    node_weight,
    mix_weight,
    latent_in,
    latent_out,
    readout,
    species_scale,
    species_shift,
):
    groups, select, hot, images = lattice_plan(sizes[2])
    rows = hot.shape[1]
    slots = images.shape[1]
    ch = mix_weight.shape[0]
    hid = latent_in.shape[1]
    count = len(groups)
    faces = sum(whole_face(o) for o in groups)
    operands = {
        "node": node_weight,
        "attr": attributes,
        "pos": positions,
        "occ": occupied.reshape(1, SITES),
        "species": species.reshape(1, SITES),
        "scale": species_scale.reshape(1, -1),
        "shift": species_shift.reshape(1, -1),
        "slots": site_slots.reshape(1, SITES),
        "select": jnp.asarray(select[SITES:], dtype=BF16),
        "hot": jnp.asarray(hot, dtype=BF16),
        "images": jnp.asarray(images),
        "radial": radial_weight,
        "mix": mix_weight,
        "latent_in": latent_in,
        "latent_out": latent_out.T,
        "readout": readout.reshape(1, ch),
    }
    names = tuple(operands)
    dma = pltpu.SemaphoreType.DMA
    per_slot = lambda *dims: pltpu.VMEM((slots,) + dims + (SITES,), F32)
    energy, forces = pl.pallas_call(
        functools.partial(brick_kernel, groups, sizes, rows, slots, ch, names),
        out_shape=(
            jax.ShapeDtypeStruct((1, SITES), F32),
            jax.ShapeDtypeStruct((3, SITES), F32),
        ),
        in_specs=[ANY] * len(names),
        out_specs=(VMEM, VMEM),
        scratch_shapes=[pltpu.VMEM(v.shape, v.dtype) for v in operands.values()]
        + [
            dma((len(names),)),
            pltpu.VMEM((ch + 8, SITES), F32),
            pltpu.VMEM((faces, ch + 8, SITES), F32),
            pltpu.VMEM((rows - SITES, SITES), F32),
            pltpu.VMEM((rows - SITES, SITES), F32),
            dma((count,)),
            dma((count,)),
            pltpu.VMEM((rows // SITES, 8, SITES), F32),
            pltpu.VMEM((count, 8, SITES), F32),
            dma((count,)),
            dma((count,)),
            pltpu.VMEM((2 * ch + 32, rows), BF16),
            per_slot(ch),
            per_slot(8),
            per_slot(8),
            per_slot(16),
            per_slot(),
            per_slot(ch),
            per_slot(ch),
            per_slot(ch),
            per_slot(ch),
            pltpu.VMEM((9, ch, SITES), F32),
            pltpu.VMEM((9, ch, SITES), F32),
            per_slot(3 * ch),
            per_slot(ch),
            per_slot(ch),
            per_slot(),
            per_slot(8),
            per_slot(16),
            per_slot(16),
            pltpu.VMEM((hid, 12 * ch), BF16),
            pltpu.VMEM((4 * ch, 3 * hid), BF16),
        ],
        compiler_params=pltpu.CompilerParams(
            collective_id=0, has_side_effects=True, vmem_limit_bytes=56 * 2**20
        ),
        name="brick",
    )(*operands.values())
    return (energy.reshape(SITES), forces)


def solution(mesh):
    sizes = tuple(mesh.shape[a] for a in AXES)
    return jax.shard_map(
        functools.partial(shards, sizes),
        mesh=mesh,
        in_specs=(
            P(None, AXES),
            P(None, AXES),
            P(AXES),
            P(AXES),
            P(None, AXES),
            P(None, AXES),
            P(AXES),
            P(),
            P(),
            P(),
            P(),
            P(),
            P(),
            P(),
            P(),
        ),
        out_specs=(P(AXES), P(None, AXES)),
        check_vma=False,
    )
```
